128 devices in a mesh: batch: 16 (over x, y), proto: 8 (over z, core).
Axes of the slice: x: 4, y: 4, z: 4, core: 2. Of those that a mesh axis runs over, the one named last changes fastest.
Arguments:
- features: bfloat16 [10, 1024, 256], P(None, 'batch'), may hold values from -6 to 6
- teacher_logits: bfloat16 [2, 1024, 65536], P(None, 'batch', 'proto'), may hold values from -12 to 12
- directions: bfloat16 [256, 65536], P(None, 'proto'), may hold values from -0.375 to 0.375
- center: float32 [65536], P('proto'), may hold values from -3 to 3
Outputs:
- grad_features: float32 [10, 1024, 256], P(None, 'batch')
- grad_directions: float32 [256, 65536], P('batch', 'proto')
- new_center: float32 [65536], P('proto')
The draws below stay inside these ranges and needn't reach their ends.
All inputs are finite; a program needn't handle non-finite values.
Results may differ from the reference program's by a relative error of at most 0.0003.
The reference program's roundings to bfloat16 on the way count: a program that leaves them out, or rounds other values in their place, can miss the bound.
Values sent between devices are 32-bit elements; how exact they have to be, the bound alone decides.
No kernel may reach another device: no remote copies, remote signals or barrier semaphores. Data moves between devices by JAX's collectives and lax.ppermute only.
A program may use at most 128 MiB of HBM per device.

```python
import jax
import jax.numpy as jnp
from jax import lax

D = 256
PROTOS = 65536
GLOBAL = 2
LOCAL = 8
IMG_DEV = 64
IMAGES = 1024
N_BATCH = 16


def draw_teacher_logits(key, part):
    key = jax.random.fold_in(key, 11)
    keys = jax.random.split(key, 2)
    place = jnp.arange(IMAGES, dtype=jnp.float32) / IMAGES
    rising = (0.5 + 1.5 * place)[None, :, None]
    col_off = 0.3 * jax.random.normal(keys[1], (PROTOS,), jnp.float32)
    base = 0.15 * jax.random.normal(keys[0], (GLOBAL, IMAGES, PROTOS), jnp.float32)
    value = base * rising + col_off
    return jnp.clip(value, -12.0, 12.0).astype(jnp.bfloat16)


def spiked(drawn, stream_key, source, target, blocks, factor):
    owner, partner = [(jnp.arange(drawn.shape[position]) // (drawn.shape[position] // blocks)).reshape([-1 if axis == position else 1 for axis in range(drawn.ndim)]) for position in (source, target)]
    chosen = jax.random.permutation(stream_key, blocks)[partner]
    strong = (owner == chosen) | (owner == (partner + blocks // 2) % blocks)
    return jnp.where(strong, factor * drawn, drawn)


def block_scale(key, dims, cuts, smallest, top_value):
    def one(position, shards_of):
        steps = jax.random.uniform(jax.random.fold_in(jax.random.fold_in(key, 6), position), (shards_of,), jnp.float32, smallest / len(cuts), top_value / len(cuts))
        return jnp.repeat(jnp.exp(steps), dims[position] // shards_of).reshape((-1,) + (1,) * (len(dims) - position - 1))

    level = one(*cuts[0])
    for cut in cuts[1:]:
        level = level * one(*cut)
    return level


def gaussian(own_key, shape, scale, limit, shards=(), held_as=jnp.bfloat16):
    result = jax.random.normal(own_key, shape, jnp.float32) * scale
    if len(shards) > 0:
        result = block_scale(own_key, shape, shards, -0.22, 0.18) * result
    return jnp.clip(result, min=-limit, max=limit).astype(held_as)


def bell_draw_with(own_key, extent, width, most, shards, heavy, held_as=jnp.bfloat16):
    result = width * jax.random.normal(own_key, extent, jnp.float32)
    if shards:
        result = result * block_scale(own_key, extent, shards, -0.22, 0.18)
    return jnp.clip(spiked(result, jax.random.fold_in(own_key, 3), *heavy), -most, most).astype(held_as)


def setup_inputs(seed: int = 0) -> dict:
    splits = jax.random.split(jax.random.key(seed), 5)
    return {
        "features": bell_draw_with(splits[0], (GLOBAL + LOCAL, IMAGES, D), 1.0, 6.0, ((1, 16),), (1, 2, 16, 2.0)),
        "teacher_logits": draw_teacher_logits(jax.random.fold_in(splits[4], 71), 0),
        "directions": gaussian(splits[2], (D, PROTOS), D ** -0.5, 0.375, ((1, 8),)),
        "center": gaussian(splits[3], (PROTOS,), 0.3, 3.0, ((0, 8),), jnp.float32),
    }


def reference(features, teacher_logits, directions, center):
    dirs = directions.astype(jnp.float32)
    col_norm = jnp.sqrt(lax.optimization_barrier(jnp.sum(dirs * dirs, axis=0)) + 1e-06)
    weight = dirs / col_norm
    weight_b = weight.astype(jnp.bfloat16)
    crops = GLOBAL + LOCAL
    counts = jnp.concatenate([jnp.ones((GLOBAL,), jnp.float32), 2.0 * jnp.ones((LOCAL,), jnp.float32)])
    scale = 1.0 / (0.1 * 18.0 * IMAGES)
    feat_blocks = features.reshape(crops, N_BATCH, IMG_DEV, D).transpose(1, 0, 2, 3)
    teach_blocks = teacher_logits.reshape(GLOBAL, N_BATCH, IMG_DEV, PROTOS).transpose(1, 0, 2, 3)

    def block(carry, inputs):
        feats, teach = inputs
        zf = feats.astype(jnp.float32)
        inv_norm = 1.0 / jnp.sqrt(lax.optimization_barrier(jnp.sum(zf * zf, axis=-1, keepdims=True)) + 1e-06)
        unit = zf * inv_norm
        unit_b = unit.astype(jnp.bfloat16)
        scores = jnp.einsum('cbd,dp->cbp', unit_b.astype(jnp.float32), weight_b.astype(jnp.float32)) / 0.1
        student = jax.nn.softmax(scores, axis=-1)
        teacher = jax.nn.softmax((teach.astype(jnp.float32) - center) / 0.04, axis=-1)
        both = teacher[0] + teacher[1]
        target = jnp.concatenate([teacher[1][None], teacher[0][None], jnp.broadcast_to(both, (LOCAL,) + both.shape)], axis=0)
        grad_b = ((counts[:, None, None] * student - target) * scale).astype(jnp.bfloat16)
        grad_weight = carry + jnp.einsum('cbd,cbp->dp', unit_b.astype(jnp.float32), grad_b.astype(jnp.float32))
        grad_unit = jnp.einsum('cbp,dp->cbd', grad_b.astype(jnp.float32), weight_b.astype(jnp.float32))
        grad_feat = (grad_unit - unit * lax.optimization_barrier(jnp.sum(grad_unit * unit, axis=-1, keepdims=True))) * inv_norm
        return (grad_weight, grad_feat)
    grad_weight, grad_blocks = lax.scan(block, jnp.zeros((D, PROTOS), jnp.float32), (feat_blocks, teach_blocks))
    grad_features = grad_blocks.transpose(1, 0, 2, 3).reshape(crops, IMAGES, D)
    grad_directions = (grad_weight - weight * lax.optimization_barrier(jnp.sum(grad_weight * weight, axis=0))) / col_norm
    col_sums = lax.optimization_barrier(jnp.sum(teacher_logits.astype(jnp.float32), axis=(0, 1)))
    new_center = 0.9 * center + 0.1 * col_sums / (2.0 * IMAGES)
    return (grad_features, grad_directions, new_center)
```

```python
import functools
import math

import jax
import jax.numpy as jnp
from jax import lax
from jax.experimental import pallas as pl
from jax.experimental.pallas import tpu as pltpu
from jax.sharding import PartitionSpec as P

F32 = jnp.float32
BF16 = jnp.bfloat16
LOG2E = math.log2(math.e)
STUDENT_C = 10.0 * LOG2E
TEACHER_C = 25.0 * LOG2E
EPS = 1e-06
VMEM = 56 * 1024 * 1024
CHUNKS = 2
STAT_TILE = 1024
TILE = 256


def stats_kernel(
    f_ref, dir_ref, t_ref, c_ref, ub_ref, inv_ref, colsum_ref, stat_ref, sacc, macc, tacc
):
    step = pl.program_id(0)
    rows = f_ref.shape[0]

    @pl.when(step == 0)
    def _():
        zf = f_ref[...].astype(F32)
        inv = 1.0 / jnp.sqrt(jnp.sum(zf * zf, axis=-1, keepdims=True) + EPS)
        ub_ref[...] = (zf * inv).astype(BF16)
        sacc[...] = jnp.zeros_like(sacc)
        macc[...] = jnp.full_like(macc, -1e30)
        tacc[...] = jnp.zeros_like(tacc)

    d = dir_ref[...].astype(F32)
    inv_col = 1.0 / jnp.sqrt(jnp.sum(d * d, axis=0, keepdims=True) + EPS)
    inv_ref[...] = inv_col
    wb = (d * inv_col).astype(BF16)
    width = d.shape[1]
    ub = ub_ref[...]
    for k in range(width // TILE):
        s = jnp.dot(ub, wb[:, k * TILE : (k + 1) * TILE], preferred_element_type=F32)
        e = jnp.exp2(s * STUDENT_C)
        part = e[:, :128]
        for m in range(1, TILE // 128):
            part += e[:, m * 128 : (m + 1) * 128]
        sacc[...] += part
    t = t_ref[...].astype(F32)
    colsum_ref[...] = jnp.sum(t, axis=0, keepdims=True)
    diff = t - c_ref[...]
    lanes = [diff[:, m * 128 : (m + 1) * 128] for m in range(width // 128)]
    old = macc[...]
    top = functools.reduce(jnp.maximum, lanes, old)
    total = tacc[...] * jnp.exp2((old - top) * TEACHER_C)
    for lane in lanes:
        total += jnp.exp2((lane - top) * TEACHER_C)
    macc[...] = top
    tacc[...] = total

    @pl.when(step == pl.num_programs(0) - 1)
    def _():
        stat_ref[...] = jnp.zeros_like(stat_ref)
        for r in range(rows // 128):
            stat_ref[r : r + 1, :] = jnp.sum(
                sacc[r * 128 : (r + 1) * 128, :].T, axis=0, keepdims=True
            )
        tops = macc[...].T
        best = jnp.max(tops, axis=0, keepdims=True)
        stat_ref[5:6, :] = best
        stat_ref[6:7, :] = jnp.sum(
            tacc[...].T * jnp.exp2((tops - best) * TEACHER_C), axis=0, keepdims=True
        )


def grad_kernel(images, place, stat_ref, f_ref, ub_ref, *refs):
    first = place[3] == 0
    del first
    (dirs, invs, teach, cents) = (refs[0:4], refs[4:8], refs[8:12], refs[12:16])
    (before_ref, xp, xm, xk, yp, ym, yk, after_ref, keep_ref, send_ref) = refs[16:26]
    (utx, uty, tflat, arow, brow, mrow, acc, gbuf, wbuf) = refs[26:35]
    step = pl.program_id(0)
    x, y, core = place[0], place[1], place[2]
    rows = ub_ref.shape[0]
    img = rows // 10
    scale = 1.0 / (0.1 * 18.0 * images)

    def block_of(xr, yr):
        return pl.multiple_of(lax.rem(x + xr, 4) * 64 + lax.rem(y + yr, 4) * 16, 16)

    @pl.when(step == 0)
    def _():
        tflat[...] = ub_ref[...].T
        for a in range(4):
            for b in range(4):
                at = (a * 4 + b) * 16
                utx[at : at + 16, :] = tflat[pl.ds(block_of(a, b), 16), :]
                uty[at : at + 16, :] = tflat[pl.ds(block_of(b, a), 16), :]
        stat = stat_ref[...]
        sums = jnp.sum(stat, axis=0)
        top = jnp.max(stat[:, 5:6, :], axis=0)
        ttot = jnp.sum(stat[:, 6:7, :] * jnp.exp2((stat[:, 5:6, :] - top) * TEACHER_C), axis=0)
        packed = jnp.concatenate([sums[0:5], top, ttot, jnp.zeros((121, 128), F32)], axis=0).T
        for r in range(5):
            arow[r * 128 : (r + 1) * 128, :] = jnp.broadcast_to(
                scale / packed[:, r : r + 1], (128, 128)
            )
        arow[2 * img :, :] = 2.0 * arow[2 * img :, :]
        mrow[...] = jnp.broadcast_to(packed[:, 5:6], (128, 128))
        brow[...] = jnp.broadcast_to(scale / packed[:, 6:7], (128, 128))
        acc[...] = before_ref[...]

    ub = ub_ref[...]
    for q in range(4):
        cols = slice(q * TILE, (q + 1) * TILE)
        inv = invs[q][...]
        wb = (dirs[q][...].astype(F32) * inv).astype(BF16)
        wbuf[:, cols] = wb
        s = jnp.dot(ub, wb, preferred_element_type=F32)
        for m in range(TILE // 128):
            lane = slice(m * 128, (m + 1) * 128)
            diff = teach[q][:, lane].astype(F32) - cents[q][:, lane]
            t = jnp.exp2((diff - mrow[...]) * TEACHER_C) * brow[...]
            t0, t1 = t[:img], t[img:]
            both = t0 + t1
            for j in range(10):
                r = slice(j * img, (j + 1) * img)
                target = t1 if j == 0 else t0 if j == 1 else both
                g = jnp.exp2(s[r, lane] * STUDENT_C) * arow[r, :] - target
                gbuf[r, q * TILE + m * 128 : q * TILE + (m + 1) * 128] = g.astype(BF16)
        ut = utx if q < 2 else uty
        gw = jnp.dot(ut[...], gbuf[:, cols], preferred_element_type=F32)
        weights = []
        dots = jnp.zeros((1, TILE), F32)
        for a in range(4):
            for b in range(4):
                at = (a * 4 + b) * 16
                start = block_of(a, b) if q < 2 else block_of(b, a)
                w = dirs[q][pl.ds(start, 16), :].astype(F32) * inv
                weights.append(w)
                dots += jnp.sum(gw[at : at + 16] * w, axis=0, keepdims=True)
        plus, minus, kept = (xp, xm, xk) if q < 2 else (yp, ym, yk)
        even = q % 2 == 0
        where = (
            [(kept, 128), (kept, 0), (plus, 0), (minus, 64)]
            if even
            else [(kept, 192), (plus, 64), (minus, 0), (kept, 64)]
        )
        for a in range(4):
            ref, base = where[a]
            for b in range(4):
                at = (a * 4 + b) * 16
                ref[base + b * 16 : base + (b + 1) * 16, :] = (
                    gw[at : at + 16] - weights[a * 4 + b] * dots
                ) * inv
    acc[...] += lax.dot_general(
        gbuf[...], wbuf[...], (((1,), (1,)), ((), ())), preferred_element_type=F32
    )

    @pl.when(step == pl.num_programs(0) - 1)
    def _():
        g = acc[...]
        after_ref[...] = g
        zf = f_ref[...].astype(F32)
        inv = 1.0 / jnp.sqrt(jnp.sum(zf * zf, axis=-1, keepdims=True) + EPS)
        unit = zf * inv
        acc[...] = (g - unit * jnp.sum(g * unit, axis=-1, keepdims=True)) * inv
        half = rows // 2
        keep_ref[...] = acc[pl.ds(pl.multiple_of(core * half, 8), half), :]
        send_ref[...] = acc[pl.ds(pl.multiple_of((1 - core) * half, 8), half), :]


def stats_call(f, dirs, teach, center):
    rows, dim = f.shape
    protos = dirs.shape[1]
    trows = teach.shape[0]
    whole = lambda i: (0, 0)
    tile = lambda i: (0, i)
    return pl.pallas_call(
        stats_kernel,
        grid=(protos // STAT_TILE,),
        in_specs=[
            pl.BlockSpec((rows, dim), whole),
            pl.BlockSpec((dim, STAT_TILE), tile),
            pl.BlockSpec((trows, STAT_TILE), tile),
            pl.BlockSpec((1, STAT_TILE), tile),
        ],
        out_specs=[
            pl.BlockSpec((rows, dim), whole),
            pl.BlockSpec((1, STAT_TILE), tile),
            pl.BlockSpec((1, STAT_TILE), tile),
            pl.BlockSpec((8, 128), whole),
        ],
        out_shape=[
            jax.ShapeDtypeStruct((rows, dim), BF16),
            jax.ShapeDtypeStruct((1, protos), F32),
            jax.ShapeDtypeStruct((1, protos), F32),
            jax.ShapeDtypeStruct((8, 128), F32),
        ],
        scratch_shapes=[
            pltpu.VMEM((rows, 128), F32),
            pltpu.VMEM((trows, 128), F32),
            pltpu.VMEM((trows, 128), F32),
        ],
        compiler_params=pltpu.CompilerParams(
            dimension_semantics=("arbitrary",), vmem_limit_bytes=VMEM
        ),
        cost_estimate=pl.CostEstimate(
            flops=2 * rows * dim * protos,
            bytes_accessed=2 * (dim + trows) * protos,
            transcendentals=(rows + trows) * protos,
        ),
        name="stats",
    )(f, dirs, teach, center)


def grad_call(images, chunk, place, stat, f, ub, dirs, inv, teach, center, before):
    rows, dim = f.shape
    protos = dirs.shape[1]
    trows = teach.shape[0]
    quarter = protos // 4
    part = quarter // CHUNKS
    steps = part // TILE
    whole = lambda i, p: (0, 0)
    tile = lambda i, p: (0, i)

    def at(q):
        base = (q * quarter + chunk * part) // TILE
        return lambda i, p: (0, base + i)

    spread = lambda height: [pl.BlockSpec((height, TILE), at(q)) for q in range(4)]
    half = rows // 2
    out = lambda height: jax.ShapeDtypeStruct((height, part), F32)
    return pl.pallas_call(
        functools.partial(grad_kernel, images),
        grid_spec=pltpu.PrefetchScalarGridSpec(
            num_scalar_prefetch=1,
            grid=(steps,),
            in_specs=[
                pl.BlockSpec((8, 8, 128), lambda i, p: (0, 0, 0)),
                pl.BlockSpec((rows, dim), whole),
                pl.BlockSpec((rows, dim), whole),
            ]
            + spread(dim)
            + spread(1)
            + spread(trows)
            + spread(1)
            + [pl.BlockSpec((rows, dim), whole)],
            out_specs=[
                pl.BlockSpec((128, TILE), tile),
                pl.BlockSpec((128, TILE), tile),
                pl.BlockSpec((256, TILE), tile),
                pl.BlockSpec((128, TILE), tile),
                pl.BlockSpec((128, TILE), tile),
                pl.BlockSpec((256, TILE), tile),
                pl.BlockSpec((rows, dim), whole),
                pl.BlockSpec((half, dim), whole),
                pl.BlockSpec((half, dim), whole),
            ],
            scratch_shapes=[
                pltpu.VMEM((dim, rows), BF16),
                pltpu.VMEM((dim, rows), BF16),
                pltpu.VMEM((dim, rows), BF16),
                pltpu.VMEM((rows, 128), F32),
                pltpu.VMEM((trows, 128), F32),
                pltpu.VMEM((trows, 128), F32),
                pltpu.VMEM((rows, dim), F32),
                pltpu.VMEM((rows, 4 * TILE), BF16),
                pltpu.VMEM((dim, 4 * TILE), BF16),
            ],
        ),
        out_shape=[out(128), out(128), out(256), out(128), out(128), out(256)]
        + [
            jax.ShapeDtypeStruct((rows, dim), F32),
            jax.ShapeDtypeStruct((half, dim), F32),
            jax.ShapeDtypeStruct((half, dim), F32),
        ],
        compiler_params=pltpu.CompilerParams(
            dimension_semantics=("arbitrary",), vmem_limit_bytes=VMEM
        ),
        cost_estimate=pl.CostEstimate(
            flops=6 * rows * dim * protos // CHUNKS,
            bytes_accessed=(2 * (dim + trows) + 4 * dim) * protos // CHUNKS,
            transcendentals=(rows + trows) * protos // CHUNKS,
        ),
        name="grads",
    )(place, stat, f, ub, *([dirs] * 4), *([inv] * 4), *([teach] * 4), *([center] * 4), before)


def shift_x(d):
    return [(x * 4 + y, ((x + d) % 4) * 4 + y) for x in range(4) for y in range(4)]


def shift_y(d):
    return [(x * 4 + y, x * 4 + (y + d) % 4) for x in range(4) for y in range(4)]


def ring(plus, minus, kept, shift):
    n = plus.shape[0] // 2
    up = lax.ppermute(plus, "batch", shift(1))
    down = lax.ppermute(minus, "batch", shift(-1))
    up2 = lax.ppermute(up[:n] + kept[:n], "batch", shift(1))
    down2 = lax.ppermute(down[:n] + kept[n : 2 * n], "batch", shift(-1))
    first = kept[2 * n : 3 * n] + down[n:] + up2
    second = kept[3 * n :] + up[n:] + down2
    return first, second


def second_ring(first, second, shift):
    n = first.shape[0] // 4
    f = [first[n * k : n * (k + 1)] for k in range(4)]
    s = [second[n * k : n * (k + 1)] for k in range(4)]
    plus = jnp.concatenate([f[2], s[1]], axis=0)
    minus = jnp.concatenate([s[2], f[3]], axis=0)
    kept = jnp.concatenate([f[1], s[3], f[0], s[0]], axis=0)
    return ring(plus, minus, kept, shift)


def on_device(features, teacher_logits, directions, center):
    crops, img, dim = features.shape
    images = img * lax.axis_size("batch")
    protos = directions.shape[1]
    rows = crops * img
    f = features.reshape(rows, dim)
    teach = teacher_logits.reshape(-1, protos)
    cent = center.reshape(1, protos)
    b, p = lax.axis_index("batch"), lax.axis_index("proto")
    place = jnp.stack([b // 4, b % 4, p % 2, 0]).astype(jnp.int32)
    ub, inv, colsum, stat = stats_call(f, directions, teach, cent)
    col_sums = lax.psum(colsum.reshape(protos), "batch")
    new_center = 0.9 * center + 0.1 * col_sums / (2.0 * images)
    stats = lax.all_to_all(jnp.broadcast_to(stat, (8, 8, 128)), "proto", 0, 0)
    before = jnp.zeros((rows, dim), F32)
    pieces = [[] for _ in range(4)]
    for chunk in range(CHUNKS):
        xp, xm, xk, yp, ym, yk, before, keep, send = grad_call(
            images, chunk, place, stats, f, ub, directions, inv, teach, cent, before
        )
        out_x = second_ring(*ring(xp, xm, xk, shift_x), shift_y)
        out_y = second_ring(*ring(yp, ym, yk, shift_y), shift_x)
        for q, piece in enumerate(out_x + out_y):
            pieces[q].append(piece)
    grad_directions = jnp.concatenate([part for row in pieces for part in row], axis=1)
    total = keep + lax.ppermute(send, "proto", [(i, i ^ 1) for i in range(8)])
    total = total + lax.ppermute(total, "proto", [(i, i ^ 2) for i in range(8)])
    total = total + lax.ppermute(total, "proto", [(i, 6 - 2 * (i // 2) + i % 2) for i in range(8)])
    other = lax.ppermute(total, "proto", [(i, i ^ 1) for i in range(8)])
    even = p % 2 == 0
    grad_features = jnp.concatenate(
        [jnp.where(even, total, other), jnp.where(even, other, total)], axis=0
    ).reshape(crops, img, dim)
    return (grad_features, grad_directions, new_center)


def solution(mesh):
    in_specs = (P(None, "batch", None), P(None, "batch", "proto"), P(None, "proto"), P("proto"))
    out_specs = (P(None, "batch", None), P("batch", "proto"), P("proto"))
    return jax.shard_map(
        on_device, mesh=mesh, in_specs=in_specs, out_specs=out_specs, check_vma=False
    )
```

```python
import functools
import math

import jax
import jax.numpy as jnp
from jax import lax
from jax.experimental import pallas as pl
from jax.experimental.pallas import tpu as pltpu
from jax.sharding import PartitionSpec as P

F32 = jnp.float32
BF16 = jnp.bfloat16
STUDENT_C = 10.0 * math.log2(math.e)
TEACHER_C = 25.0
EPS = 1e-06
PARTS = 4
CALLS = 2
STAT_TILE = 1024
STAT_SUB = 256
SUB = 512

_KEEP = {0: (0, 3), 1: (0, 1), 2: (0, 3), 3: (0, 1)}
_SEND = {0: (1, 2), 1: (3, 2), 2: (1, 2), 3: (3, 2)}


def blocks_of(part):
    outer = _KEEP[part] + _SEND[part]
    if part < 2:
        return [(a, b) for a in outer for b in outer]
    return [(b, a) for a in outer for b in outer]


def block_start(kx, ky):
    place = lax.axis_index("batch")
    x, y = lax.div(place, 4), lax.rem(place, 4)
    return pl.multiple_of(lax.bitwise_xor(x, kx) * 64 + lax.bitwise_xor(y, ky) * 16, 16)


def stats_kernel(
    f_ref, c_ref, dir_hbm, t_hbm, ub_ref, ut_ref, inv_ref, colsum_ref, stat_ref,
    dbuf, tbuf, sacc, macc, tacc, dsem, tsem,
):
    rows = f_ref.shape[0]
    protos = dbuf.shape[1]
    tiles = protos // STAT_TILE

    def copies(n):
        cols = pl.ds(pl.multiple_of(n * STAT_TILE, STAT_TILE), STAT_TILE)
        return (
            pltpu.make_async_copy(dir_hbm.at[:, cols], dbuf.at[:, cols], dsem.at[n]),
            pltpu.make_async_copy(t_hbm.at[:, cols], tbuf.at[:, cols], tsem.at[n]),
        )

    for n in range(tiles):
        for copy in copies(n):
            copy.start()
    zf = f_ref[...].astype(F32)
    inv = 1.0 / jnp.sqrt(jnp.sum(zf * zf, axis=-1, keepdims=True) + EPS)
    ub = (zf * inv).astype(BF16)
    ub_ref[...] = ub
    ut_ref[...] = ub.T
    sacc[...] = jnp.zeros_like(sacc)
    macc[...] = jnp.full_like(macc, -1e30)
    tacc[...] = jnp.zeros_like(tacc)
    colsum_ref[...] = jnp.zeros_like(colsum_ref)

    @pl.loop(0, tiles)
    def _(n):
        for copy in copies(n):
            copy.wait()
        cols = pl.ds(pl.multiple_of(n * STAT_TILE, STAT_TILE), STAT_TILE)
        d = dbuf[:, cols].astype(F32)
        inv_col = 1.0 / jnp.sqrt(jnp.sum(d * d, axis=0, keepdims=True) + EPS)
        inv_ref[:, cols] = inv_col
        wb = (d * inv_col).astype(BF16)
        part = None
        for k in range(STAT_TILE // STAT_SUB):
            s = jnp.dot(
                ub_ref[...], wb[:, k * STAT_SUB : (k + 1) * STAT_SUB], preferred_element_type=F32
            )
            e = jnp.exp2(s * STUDENT_C)
            for m in range(STAT_SUB // 128):
                lane = e[:, m * 128 : (m + 1) * 128]
                part = lane if part is None else part + lane
        sacc[...] += part
        t = tbuf[:, cols].astype(F32)
        colsum_ref[pl.ds(n, 1), :] = jnp.sum(t, axis=0, keepdims=True)
        diff = t - c_ref[:, cols]
        lanes = [diff[:, m * 128 : (m + 1) * 128] for m in range(STAT_TILE // 128)]
        old = macc[...]
        top = functools.reduce(jnp.maximum, lanes, old)
        total = tacc[...] * jnp.exp((old - top) * TEACHER_C)
        for lane in lanes:
            total += jnp.exp((lane - top) * TEACHER_C)
        macc[...] = top
        tacc[...] = total

    stat_ref[...] = jnp.zeros_like(stat_ref)
    for r in range(rows // 128):
        stat_ref[r : r + 1, :] = jnp.sum(sacc[r * 128 : (r + 1) * 128, :].T, axis=0, keepdims=True)
    tops = macc[...].T
    best = jnp.max(tops, axis=0, keepdims=True)
    stat_ref[5:6, :] = best
    stat_ref[6:7, :] = jnp.sum(
        tacc[...].T * jnp.exp((tops - best) * TEACHER_C), axis=0, keepdims=True
    )


def weight_kernel(images, call, *refs):
    refs = list(refs)
    take = lambda n: [refs.pop(0) for _ in range(n)]
    first, last = call == 0, call == CALLS - 1
    ub_ref, ut_ref, dir_ref, inv_ref, t_ref, c_ref = take(6)
    stat_ref, colsum_ref = take(2) if first else (None, None)
    arow, brow, mrow, before_ref = take(4) if not first else (None,) * 4
    (f_ref,) = take(1) if last else (None,)
    keep_refs, send_refs = take(PARTS), take(PARTS)
    fouts = take(2 if last else 1)
    rows = ub_ref.shape[0]
    img = rows // 10
    if first:
        arow, brow, mrow = take(3)
        scale = 1.0 / (0.1 * 18.0 * images)
        stat = stat_ref[...]
        sums = jnp.sum(stat, axis=0)
        top = jnp.max(stat[:, 5:6, :], axis=0)
        ttot = jnp.sum(stat[:, 6:7, :] * jnp.exp((stat[:, 5:6, :] - top) * TEACHER_C), axis=0)
        packed = jnp.concatenate([sums[0:5], top, ttot, jnp.zeros((121, 128), F32)], axis=0).T
        for r in range(5):
            arow[r * 128 : (r + 1) * 128, :] = jnp.broadcast_to(
                (scale if r == 0 else 2.0 * scale) / packed[:, r : r + 1], (128, 128)
            )
        mrow[...] = jnp.broadcast_to(packed[:, 5:6], (128, 128))
        brow[...] = jnp.broadcast_to(scale / packed[:, 6:7], (128, 128))
    ub = ub_ref[...]
    protos = dir_ref.shape[1]
    width = protos // PARTS // CALLS
    wide = lambda v: jnp.concatenate([v] * (SUB // 128), axis=1)
    total = None
    for part in range(PARTS):
        ut = jnp.concatenate(
            [ut_ref[pl.ds(block_start(kx, ky), 16), :] for kx, ky in blocks_of(part)], axis=0
        )
        base = (part * CALLS + call) * width
        for at in range(0, width, SUB):
            cols, mine = slice(at, at + SUB), slice(base + at, base + at + SUB)
            inv = inv_ref[:, mine]
            wb = (dir_ref[:, mine].astype(F32) * inv).astype(BF16)
            s = jnp.dot(ub, wb, preferred_element_type=F32)
            diff = t_ref[:, mine].astype(F32) - c_ref[:, mine]
            t = jnp.exp((diff - wide(mrow[...])) * TEACHER_C) * wide(brow[...])
            t0, t1 = t[:img], t[img:]
            both = t0 + t1
            rounded = []
            for j in range(10):
                r = slice(j * img, (j + 1) * img)
                target = t1 if j == 0 else t0 if j == 1 else both
                rounded.append(
                    (jnp.exp2(s[r] * STUDENT_C) * wide(arow[r, :]) - target).astype(BF16)
                )
            g = jnp.concatenate(rounded, axis=0)
            gw = jnp.dot(ut, g, preferred_element_type=F32)
            term = lax.dot_general(g, wb, (((1,), (1,)), ((), ())), preferred_element_type=F32)
            total = term if total is None else total + term
            ds = []
            dots = jnp.zeros((16, SUB), F32)
            for n, (kx, ky) in enumerate(blocks_of(part)):
                d = dir_ref[pl.ds(block_start(kx, ky), 16), mine].astype(F32)
                ds.append(d)
                dots += gw[n * 16 : (n + 1) * 16] * d
            factor = jnp.sum(dots, axis=0, keepdims=True) * inv * inv * inv
            for n in range(16):
                ref, row = (keep_refs[part], n * 16) if n < 8 else (send_refs[part], (n - 8) * 16)
                ref[row : row + 16, cols] = gw[n * 16 : (n + 1) * 16] * inv - ds[n] * factor
    if first:
        send_refs[0][128:136, :] = colsum_ref[...]
    else:
        total = before_ref[...] + total
    if not last:
        fouts[0][...] = total
        return
    (acc,) = take(1)
    zf = f_ref[...].astype(F32)
    inv = 1.0 / jnp.sqrt(jnp.sum(zf * zf, axis=-1, keepdims=True) + EPS)
    unit = zf * inv
    acc[...] = (total - unit * jnp.sum(total * unit, axis=-1, keepdims=True)) * inv
    half = rows // 2
    core = lax.rem(lax.axis_index("proto"), 2)
    fouts[0][...] = acc[pl.ds(pl.multiple_of(core * half, 8), half), :]
    fouts[1][...] = acc[pl.ds(pl.multiple_of((1 - core) * half, 8), half), :]


def final_kernel(images, c_ref, cs_ref, csgot_ref, mine_ref, other_ref, *refs):
    keeps, gots = refs[: PARTS * CALLS], refs[PARTS * CALLS : PARTS * CALLS + PARTS]
    feat_ref, dir_ref, center_ref = refs[PARTS * CALLS + PARTS :]
    half = mine_ref.shape[0]
    core = lax.rem(lax.axis_index("proto"), 2)
    feat_ref[pl.ds(pl.multiple_of(core * half, 8), half), :] = mine_ref[...]
    feat_ref[pl.ds(pl.multiple_of((1 - core) * half, 8), half), :] = other_ref[...]
    width = keeps[0].shape[1]
    for part in range(PARTS):
        for call in range(CALLS):
            n = part * CALLS + call
            got = gots[part][call * 16 : (call + 1) * 16, :]
            dir_ref[:, n * width : (n + 1) * width] = keeps[n][...] + got
    cs = cs_ref[...] + csgot_ref[...]
    for n in range(8):
        cols = slice(n * STAT_TILE, (n + 1) * STAT_TILE)
        center_ref[:, cols] = 0.9 * c_ref[:, cols] + 0.1 * cs[n : n + 1, :] / (2.0 * images)


IN_VMEM = pl.BlockSpec(memory_space=pltpu.VMEM)


def params(mib):
    return pltpu.CompilerParams(vmem_limit_bytes=mib * 1024 * 1024)


def stats_call(f, dirs, teach, center):
    rows, dim = f.shape
    protos = dirs.shape[1]
    trows = teach.shape[0]
    tiles = protos // STAT_TILE
    return pl.pallas_call(
        stats_kernel,
        in_specs=[IN_VMEM, IN_VMEM] + [pl.BlockSpec(memory_space=pltpu.HBM)] * 2,
        out_specs=[IN_VMEM] * 5,
        scratch_shapes=[
            pltpu.VMEM((dim, protos), BF16),
            pltpu.VMEM((trows, protos), BF16),
            pltpu.VMEM((rows, 128), F32),
            pltpu.VMEM((trows, 128), F32),
            pltpu.VMEM((trows, 128), F32),
            pltpu.SemaphoreType.DMA((tiles,)),
            pltpu.SemaphoreType.DMA((tiles,)),
        ],
        out_shape=[
            jax.ShapeDtypeStruct((rows, dim), BF16),
            jax.ShapeDtypeStruct((dim, rows), BF16),
            jax.ShapeDtypeStruct((1, protos), F32),
            jax.ShapeDtypeStruct((8, STAT_TILE), F32),
            jax.ShapeDtypeStruct((8, 128), F32),
        ],
        compiler_params=params(53),
        cost_estimate=pl.CostEstimate(
            flops=2 * rows * dim * protos,
            bytes_accessed=2 * (dim + trows) * protos,
            transcendentals=(rows + trows) * protos,
        ),
        name="stats",
    )(f, center, dirs, teach)


def weight_call(images, call, ub, ut, dirs, inv, teach, center, extra):
    rows, dim = ub.shape
    protos = dirs.shape[1]
    trows = teach.shape[0]
    width = protos // PARTS // CALLS
    first, last = call == 0, call == CALLS - 1
    shape = lambda *dims: jax.ShapeDtypeStruct(dims, F32)
    outs = [shape(128, width)] * PARTS
    outs += [shape(136 if first and part == 0 else 128, width) for part in range(PARTS)]
    outs += [shape(rows // 2, dim)] * 2 if last else [shape(rows, dim)]
    outs += [shape(rows, 128), shape(trows, 128), shape(trows, 128)] if first else []
    args = [ub, ut, dirs, inv, teach, center, *extra]
    out = pl.pallas_call(
        functools.partial(weight_kernel, images, call),
        in_specs=[IN_VMEM] * len(args),
        out_specs=[IN_VMEM] * len(outs),
        scratch_shapes=[pltpu.VMEM((rows, dim), F32)] if last else [],
        out_shape=outs,
        compiler_params=params(8),
        cost_estimate=pl.CostEstimate(
            flops=6 * rows * dim * protos // CALLS,
            bytes_accessed=(2 * (dim + trows) + 4 * dim) * protos // CALLS,
            transcendentals=(rows + trows) * protos // CALLS,
        ),
        name="weights",
    )(*args)
    return out[:PARTS], out[PARTS : 2 * PARTS], out[2 * PARTS :]


def final_call(images, center, cs, csgot, mine, other, keeps, gots):
    half, dim = mine.shape
    protos = center.shape[1]
    args = [center, cs, csgot, mine, other, *keeps, *gots]
    return pl.pallas_call(
        functools.partial(final_kernel, images),
        in_specs=[IN_VMEM] * len(args),
        out_specs=[IN_VMEM] * 3,
        out_shape=[
            jax.ShapeDtypeStruct((2 * half, dim), F32),
            jax.ShapeDtypeStruct((16, protos), F32),
            jax.ShapeDtypeStruct((1, protos), F32),
        ],
        compiler_params=params(8),
        name="final",
    )(*args)


def pairs_x(k):
    return [(x * 4 + y, (x ^ k) * 4 + y) for x in range(4) for y in range(4)]


def pairs_y(k):
    return [(x * 4 + y, x * 4 + (y ^ k)) for x in range(4) for y in range(4)]


X1, X3, Y1, Y3 = pairs_x(1), pairs_x(3), pairs_y(1), pairs_y(3)
ORDER = [(X1, X3, Y1, Y3), (X3, X1, Y3, Y1), (Y1, Y3, X1, X3), (Y3, Y1, X3, X1)]


def on_device(features, teacher_logits, directions, center):
    crops, img, dim = features.shape
    images = img * lax.axis_size("batch")
    protos = directions.shape[1]
    rows = crops * img
    f = features.reshape(rows, dim)
    teach = teacher_logits.reshape(-1, protos)
    cent = center.reshape(1, protos)
    ub, ut, inv, colsum, stat = stats_call(f, directions, teach, cent)
    stats = lax.all_to_all(jnp.broadcast_to(stat, (8, 8, 128)), "proto", 0, 0)
    keeps, sends, extra = [], [], [stats, colsum]
    for call in range(CALLS):
        if call == CALLS - 1:
            extra = extra + [f]
        keep, send, rest = weight_call(images, call, ub, ut, directions, inv, teach, cent, extra)
        factors = rest[1:] if call == 0 else factors
        extra = [*factors, rest[0]]
        keeps.append(keep)
        sends.append([lax.ppermute(send[p], "batch", ORDER[p][0]) for p in range(PARTS)])
    fkeep, fsend = rest
    cs, before = colsum, None
    got = [[None] * CALLS for _ in range(PARTS)]
    for call in range(CALLS):
        for part in range(PARTS):
            block = sends[call][part]
            if before is not None:
                block, _ = lax.optimization_barrier((block, before))
            before = block
            got[part][call] = block[:128]
            if call == 0 and part == 0:
                cs = cs + block[128:]
    fsend, _ = lax.optimization_barrier((fsend, before))
    keeps = [[keeps[call][part] for call in range(CALLS)] for part in range(PARTS)]
    for n in (1, 2, 3):
        size = 128 >> n
        arrived, before = [], None
        for part in range(PARTS):
            out = [keeps[part][c][size:] + got[part][c][size:] for c in range(CALLS)]
            out += [cs] if part == 0 else []
            keeps[part] = [keeps[part][c][:size] + got[part][c][:size] for c in range(CALLS)]
            block = lax.ppermute(jnp.concatenate(out, axis=0), "batch", ORDER[part][n])
            if before is not None:
                block, _ = lax.optimization_barrier((block, before))
            before = block
            arrived.append(block)
            got[part] = [block[c * size : (c + 1) * size] for c in range(CALLS)]
        if n < 3:
            cs = cs + arrived[0][CALLS * size :]
    total = fkeep + lax.ppermute(fsend, "proto", [(i, i ^ 1) for i in range(8)])
    total = total + lax.ppermute(total, "proto", [(i, i ^ 2) for i in range(8)])
    total = total + lax.ppermute(total, "proto", [(i, i ^ 6) for i in range(8)])
    other = lax.ppermute(total, "proto", [(i, i ^ 1) for i in range(8)])
    keeps = [keeps[part][call] for part in range(PARTS) for call in range(CALLS)]
    csgot = arrived[0][CALLS * 16 :]
    grad_features, grad_directions, new_center = final_call(
        images, cent, cs, csgot, total, other, keeps, arrived
    )
    return (
        grad_features.reshape(crops, img, dim),
        grad_directions,
        new_center.reshape(protos),
    )


def solution(mesh):
    in_specs = (P(None, "batch", None), P(None, "batch", "proto"), P(None, "proto"), P("proto"))
    out_specs = (P(None, "batch", None), P("batch", "proto"), P("proto"))
    return jax.shard_map(
        on_device, mesh=mesh, in_specs=in_specs, out_specs=out_specs, check_vma=False
    )
```

```python
import functools
import math

import jax
import jax.numpy as jnp
from jax import lax
from jax.experimental import pallas as pl
from jax.experimental.pallas import tpu as pltpu
from jax.sharding import PartitionSpec as P

F32 = jnp.float32
BF16 = jnp.bfloat16
STUDENT_C = 10.0 * math.log2(math.e)
TEACHER_C = 25.0 * math.log2(math.e)
EPS = 1e-06
PARTS = 4
CALLS = 2
STAT_TILE = 1024
STAT_SUB = 1024
SUB = 512

_KEEP = {0: (0, 3), 1: (0, 1), 2: (0, 3), 3: (0, 1)}
_SEND = {0: (1, 2), 1: (3, 2), 2: (1, 2), 3: (3, 2)}


def blocks_of(part):
    outer = _KEEP[part] + _SEND[part]
    if part < 2:
        return [(a, b) for a in outer for b in outer]
    return [(b, a) for a in outer for b in outer]


def block_start(kx, ky):
    place = lax.axis_index("batch")
    x, y = lax.div(place, 4), lax.rem(place, 4)
    return pl.multiple_of(lax.bitwise_xor(x, kx) * 64 + lax.bitwise_xor(y, ky) * 16, 16)


def stats_kernel(
    f_ref, c_ref, dir_hbm, t_hbm, ub_ref, ut_ref, inv_ref, colsum_ref, stat_ref,
    dbuf, tbuf, sacc, macc, tacc, dsem, tsem,
):
    rows = f_ref.shape[0]
    protos = dbuf.shape[1]
    tiles = protos // STAT_TILE

    def copies(n):
        cols = pl.ds(pl.multiple_of(n * STAT_TILE, STAT_TILE), STAT_TILE)
        return (
            pltpu.make_async_copy(dir_hbm.at[:, cols], dbuf.at[:, cols], dsem.at[n]),
            pltpu.make_async_copy(t_hbm.at[:, cols], tbuf.at[:, cols], tsem.at[n]),
        )

    for n in range(tiles):
        for copy in copies(n):
            copy.start()
    zf = f_ref[...].astype(F32)
    inv = 1.0 / jnp.sqrt(jnp.sum(zf * zf, axis=-1, keepdims=True) + EPS)
    ub = (zf * inv).astype(BF16)
    ub_ref[...] = ub
    ut_ref[...] = ub.T
    sacc[...] = jnp.zeros_like(sacc)
    macc[...] = jnp.full_like(macc, -1e30)
    tacc[...] = jnp.zeros_like(tacc)
    colsum_ref[...] = jnp.zeros_like(colsum_ref)

    @pl.loop(0, tiles)
    def _(n):
        for copy in copies(n):
            copy.wait()
        cols = pl.ds(pl.multiple_of(n * STAT_TILE, STAT_TILE), STAT_TILE)
        d = dbuf[:, cols].astype(F32)
        inv_col = 1.0 / jnp.sqrt(jnp.sum(d * d, axis=0, keepdims=True) + EPS)
        inv_ref[:, cols] = inv_col
        wb = (d * inv_col).astype(BF16)
        part = None
        for k in range(STAT_TILE // STAT_SUB):
            s = jnp.dot(
                ub_ref[...], wb[:, k * STAT_SUB : (k + 1) * STAT_SUB], preferred_element_type=F32
            )
            e = jnp.exp2(s * STUDENT_C)
            for m in range(STAT_SUB // 128):
                lane = e[:, m * 128 : (m + 1) * 128]
                part = lane if part is None else part + lane
        sacc[...] += part
        t = tbuf[:, cols].astype(F32)
        ones = jnp.ones((8, tbuf.shape[0]), BF16)
        sums = jnp.dot(ones, tbuf[:, cols], preferred_element_type=F32)
        colsum_ref[pl.ds(n, 1), :] = sums[:1]
        diff = t - c_ref[:, cols]
        lanes = [diff[:, m * 128 : (m + 1) * 128] for m in range(STAT_TILE // 128)]
        old = macc[...]
        top = functools.reduce(jnp.maximum, lanes, old)
        total = tacc[...] * jnp.exp2((old - top) * TEACHER_C)
        for lane in lanes:
            total += jnp.exp2((lane - top) * TEACHER_C)
        macc[...] = top
        tacc[...] = total

    stat_ref[...] = jnp.zeros_like(stat_ref)
    for r in range(rows // 128):
        stat_ref[r : r + 1, :] = jnp.sum(sacc[r * 128 : (r + 1) * 128, :].T, axis=0, keepdims=True)
    tops = macc[...].T
    best = jnp.max(tops, axis=0, keepdims=True)
    stat_ref[5:6, :] = best
    stat_ref[6:7, :] = jnp.sum(
        tacc[...].T * jnp.exp2((tops - best) * TEACHER_C), axis=0, keepdims=True
    )


def weight_kernel(images, call, *refs):
    refs = list(refs)
    take = lambda n: [refs.pop(0) for _ in range(n)]
    first, last = call == 0, call == CALLS - 1
    ub_ref, ut_ref, dir_ref, inv_ref, t_ref, c_ref = take(6)
    stat_ref, colsum_ref = take(2) if first else (None, None)
    arow, brow, mrow, before_ref = take(4) if not first else (None,) * 4
    (f_ref,) = take(1) if last else (None,)
    keep_refs, send_refs = take(PARTS), take(PARTS)
    fouts = take(2 if last else 1)
    rows = ub_ref.shape[0]
    img = rows // 10
    if first:
        arow, brow, mrow = take(3)
        scale = 1.0 / (0.1 * 18.0 * images)
        stat = stat_ref[...]
        sums = jnp.sum(stat, axis=0)
        top = jnp.max(stat[:, 5:6, :], axis=0)
        ttot = jnp.sum(stat[:, 6:7, :] * jnp.exp2((stat[:, 5:6, :] - top) * TEACHER_C), axis=0)
        packed = jnp.concatenate([sums[0:5], top, ttot, jnp.zeros((121, 128), F32)], axis=0).T
        for r in range(5):
            arow[r * 128 : (r + 1) * 128, :] = jnp.broadcast_to(
                (scale if r == 0 else 2.0 * scale) / packed[:, r : r + 1], (128, 128)
            )
        mrow[...] = jnp.broadcast_to(packed[:, 5:6], (128, 128))
        brow[...] = jnp.broadcast_to(scale / packed[:, 6:7], (128, 128))
    ub = ub_ref[...]
    protos = dir_ref.shape[1]
    width = protos // PARTS // CALLS
    wide = lambda v: jnp.concatenate([v] * (SUB // 128), axis=1)
    total = None
    for part in range(PARTS):
        ut = jnp.concatenate(
            [ut_ref[pl.ds(block_start(kx, ky), 16), :] for kx, ky in blocks_of(part)], axis=0
        )
        base = (part * CALLS + call) * width
        for at in range(0, width, SUB):
            cols, mine = slice(at, at + SUB), slice(base + at, base + at + SUB)
            inv = inv_ref[:, mine]
            wb = (dir_ref[:, mine].astype(F32) * inv).astype(BF16)
            s = jnp.dot(ub, wb, preferred_element_type=F32)
            diff = t_ref[:, mine].astype(F32) - c_ref[:, mine]
            t = jnp.exp2((diff - wide(mrow[...])) * TEACHER_C) * wide(brow[...])
            t0, t1 = t[:img], t[img:]
            both = t0 + t1
            rounded = []
            for j in range(10):
                r = slice(j * img, (j + 1) * img)
                target = t1 if j == 0 else t0 if j == 1 else both
                rounded.append(
                    (jnp.exp2(s[r] * STUDENT_C) * wide(arow[r, :]) - target).astype(BF16)
                )
            g = jnp.concatenate(rounded, axis=0)
            gw = jnp.dot(ut, g, preferred_element_type=F32)
            term = lax.dot_general(g, wb, (((1,), (1,)), ((), ())), preferred_element_type=F32)
            total = term if total is None else total + term
            ds = []
            dots = jnp.zeros((16, SUB), F32)
            for n, (kx, ky) in enumerate(blocks_of(part)):
                d = dir_ref[pl.ds(block_start(kx, ky), 16), mine].astype(F32)
                ds.append(d)
                dots += gw[n * 16 : (n + 1) * 16] * d
            factor = jnp.sum(dots, axis=0, keepdims=True) * inv * inv * inv
            for n in range(16):
                ref, row = (keep_refs[part], n * 16) if n < 8 else (send_refs[part], (n - 8) * 16)
                ref[row : row + 16, cols] = gw[n * 16 : (n + 1) * 16] * inv - ds[n] * factor
    if first:
        send_refs[0][128:136, :] = colsum_ref[...]
    else:
        total = before_ref[...] + total
    if not last:
        fouts[0][...] = total
        return
    (acc,) = take(1)
    zf = f_ref[...].astype(F32)
    inv = 1.0 / jnp.sqrt(jnp.sum(zf * zf, axis=-1, keepdims=True) + EPS)
    unit = zf * inv
    acc[...] = (total - unit * jnp.sum(total * unit, axis=-1, keepdims=True)) * inv
    half = rows // 2
    core = lax.rem(lax.axis_index("proto"), 2)
    fouts[0][...] = acc[pl.ds(pl.multiple_of(core * half, 8), half), :]
    fouts[1][...] = acc[pl.ds(pl.multiple_of((1 - core) * half, 8), half), :]


def final_kernel(images, c_ref, cs_ref, csgot_ref, mine_ref, other_ref, *refs):
    keeps, gots = refs[: PARTS * CALLS], refs[PARTS * CALLS : PARTS * CALLS + PARTS]
    feat_ref, dir_ref, center_ref = refs[PARTS * CALLS + PARTS :]
    half = mine_ref.shape[0]
    core = lax.rem(lax.axis_index("proto"), 2)
    feat_ref[pl.ds(pl.multiple_of(core * half, 8), half), :] = mine_ref[...]
    feat_ref[pl.ds(pl.multiple_of((1 - core) * half, 8), half), :] = other_ref[...]
    width = keeps[0].shape[1]
    for part in range(PARTS):
        for call in range(CALLS):
            n = part * CALLS + call
            got = gots[part][call * 16 : (call + 1) * 16, :]
            dir_ref[:, n * width : (n + 1) * width] = keeps[n][...] + got
    cs = cs_ref[...] + csgot_ref[...]
    for n in range(8):
        cols = slice(n * STAT_TILE, (n + 1) * STAT_TILE)
        center_ref[:, cols] = 0.9 * c_ref[:, cols] + 0.1 * cs[n : n + 1, :] / (2.0 * images)


IN_VMEM = pl.BlockSpec(memory_space=pltpu.VMEM)


def params(mib):
    return pltpu.CompilerParams(vmem_limit_bytes=mib * 1024 * 1024)


def stats_call(f, dirs, teach, center):
    rows, dim = f.shape
    protos = dirs.shape[1]
    trows = teach.shape[0]
    tiles = protos // STAT_TILE
    return pl.pallas_call(
        stats_kernel,
        in_specs=[IN_VMEM, IN_VMEM] + [pl.BlockSpec(memory_space=pltpu.HBM)] * 2,
        out_specs=[IN_VMEM] * 5,
        scratch_shapes=[
            pltpu.VMEM((dim, protos), BF16),
            pltpu.VMEM((trows, protos), BF16),
            pltpu.VMEM((rows, 128), F32),
            pltpu.VMEM((trows, 128), F32),
            pltpu.VMEM((trows, 128), F32),
            pltpu.SemaphoreType.DMA((tiles,)),
            pltpu.SemaphoreType.DMA((tiles,)),
        ],
        out_shape=[
            jax.ShapeDtypeStruct((rows, dim), BF16),
            jax.ShapeDtypeStruct((dim, rows), BF16),
            jax.ShapeDtypeStruct((1, protos), F32),
            jax.ShapeDtypeStruct((8, STAT_TILE), F32),
            jax.ShapeDtypeStruct((8, 128), F32),
        ],
        compiler_params=params(53),
        cost_estimate=pl.CostEstimate(
            flops=2 * rows * dim * protos,
            bytes_accessed=2 * (dim + trows) * protos,
            transcendentals=(rows + trows) * protos,
        ),
        name="stats",
    )(f, center, dirs, teach)


def weight_call(images, call, ub, ut, dirs, inv, teach, center, extra):
    rows, dim = ub.shape
    protos = dirs.shape[1]
    trows = teach.shape[0]
    width = protos // PARTS // CALLS
    first, last = call == 0, call == CALLS - 1
    shape = lambda *dims: jax.ShapeDtypeStruct(dims, F32)
    outs = [shape(128, width)] * PARTS
    outs += [shape(136 if first and part == 0 else 128, width) for part in range(PARTS)]
    outs += [shape(rows // 2, dim)] * 2 if last else [shape(rows, dim)]
    outs += [shape(rows, 128), shape(trows, 128), shape(trows, 128)] if first else []
    args = [ub, ut, dirs, inv, teach, center, *extra]
    out = pl.pallas_call(
        functools.partial(weight_kernel, images, call),
        in_specs=[IN_VMEM] * len(args),
        out_specs=[IN_VMEM] * len(outs),
        scratch_shapes=[pltpu.VMEM((rows, dim), F32)] if last else [],
        out_shape=outs,
        compiler_params=params(8),
        cost_estimate=pl.CostEstimate(
            flops=6 * rows * dim * protos // CALLS,
            bytes_accessed=(2 * (dim + trows) + 4 * dim) * protos // CALLS,
            transcendentals=(rows + trows) * protos // CALLS,
        ),
        name="weights",
    )(*args)
    return out[:PARTS], out[PARTS : 2 * PARTS], out[2 * PARTS :]


def final_call(images, center, cs, csgot, mine, other, keeps, gots):
    half, dim = mine.shape
    protos = center.shape[1]
    args = [center, cs, csgot, mine, other, *keeps, *gots]
    return pl.pallas_call(
        functools.partial(final_kernel, images),
        in_specs=[IN_VMEM] * len(args),
        out_specs=[IN_VMEM] * 3,
        out_shape=[
            jax.ShapeDtypeStruct((2 * half, dim), F32),
            jax.ShapeDtypeStruct((16, protos), F32),
            jax.ShapeDtypeStruct((1, protos), F32),
        ],
        compiler_params=params(8),
        name="final",
    )(*args)


def pairs_x(k):
    return [(x * 4 + y, (x ^ k) * 4 + y) for x in range(4) for y in range(4)]


def pairs_y(k):
    return [(x * 4 + y, x * 4 + (y ^ k)) for x in range(4) for y in range(4)]


X1, X3, Y1, Y3 = pairs_x(1), pairs_x(3), pairs_y(1), pairs_y(3)
ORDER = [(X1, X3, Y1, Y3), (X3, X1, Y3, Y1), (Y1, Y3, X1, X3), (Y3, Y1, X3, X1)]


def on_device(features, teacher_logits, directions, center):
    crops, img, dim = features.shape
    images = img * lax.axis_size("batch")
    protos = directions.shape[1]
    rows = crops * img
    f = features.reshape(rows, dim)
    teach = teacher_logits.reshape(-1, protos)
    cent = center.reshape(1, protos)
    ub, ut, inv, colsum, stat = stats_call(f, directions, teach, cent)
    stats = lax.all_to_all(jnp.broadcast_to(stat, (8, 8, 128)), "proto", 0, 0)
    keeps, sends, extra = [], [], [stats, colsum]
    for call in range(CALLS):
        if call == CALLS - 1:
            extra = extra + [f]
        keep, send, rest = weight_call(images, call, ub, ut, directions, inv, teach, cent, extra)
        factors = rest[1:] if call == 0 else factors
        extra = [*factors, rest[0]]
        keeps.append(keep)
        sends.append([lax.ppermute(send[p], "batch", ORDER[p][0]) for p in range(PARTS)])
    fkeep, fsend = rest
    cs, before = colsum, None
    got = [[None] * CALLS for _ in range(PARTS)]
    for call in range(CALLS):
        for part in range(PARTS):
            block = sends[call][part]
            if before is not None:
                block, _ = lax.optimization_barrier((block, before))
            before = block
            got[part][call] = block[:128]
            if call == 0 and part == 0:
                fsend, _ = lax.optimization_barrier((fsend, block))
            if call == 0 and part == 0:
                cs = cs + block[128:]
    keeps = [[keeps[call][part] for call in range(CALLS)] for part in range(PARTS)]
    for n in (1, 2, 3):
        size = 128 >> n
        arrived, before = [], None
        for part in range(PARTS):
            out = [keeps[part][c][size:] + got[part][c][size:] for c in range(CALLS)]
            out += [cs] if part == 0 else []
            keeps[part] = [keeps[part][c][:size] + got[part][c][:size] for c in range(CALLS)]
            block = lax.ppermute(jnp.concatenate(out, axis=0), "batch", ORDER[part][n])
            if before is not None:
                block, _ = lax.optimization_barrier((block, before))
            before = block
            arrived.append(block)
            got[part] = [block[c * size : (c + 1) * size] for c in range(CALLS)]
        if n < 3:
            cs = cs + arrived[0][CALLS * size :]
    total = fkeep + lax.ppermute(fsend, "proto", [(i, i ^ 1) for i in range(8)])
    total = total + lax.ppermute(total, "proto", [(i, i ^ 2) for i in range(8)])
    total = total + lax.ppermute(total, "proto", [(i, i ^ 6) for i in range(8)])
    other = lax.ppermute(total, "proto", [(i, i ^ 1) for i in range(8)])
    keeps = [keeps[part][call] for part in range(PARTS) for call in range(CALLS)]
    csgot = arrived[0][CALLS * 16 :]
    grad_features, grad_directions, new_center = final_call(
        images, cent, cs, csgot, total, other, keeps, arrived
    )
    return (
        grad_features.reshape(crops, img, dim),
        grad_directions,
        new_center.reshape(protos),
    )


def solution(mesh):
    in_specs = (P(None, "batch", None), P(None, "batch", "proto"), P(None, "proto"), P("proto"))
    out_specs = (P(None, "batch", None), P("batch", "proto"), P("proto"))
    return jax.shard_map(
        on_device, mesh=mesh, in_specs=in_specs, out_specs=out_specs, check_vma=False
    )
```

```python
import functools
import math

import jax
import jax.numpy as jnp
from jax import lax
from jax.experimental import pallas as pl
from jax.experimental.pallas import tpu as pltpu
from jax.sharding import PartitionSpec as P

F32 = jnp.float32
BF16 = jnp.bfloat16
STUDENT_C = 10.0 * math.log2(math.e)
TEACHER_C = 25.0 * math.log2(math.e)
EPS = 1e-06
PARTS = 4
CALLS = 2
STAT_TILE = 1024
STAT_SUB = 1024
SUB = 512

_KEEP = {0: (0, 3), 1: (0, 1), 2: (0, 3), 3: (0, 1)}
_SEND = {0: (1, 2), 1: (3, 2), 2: (1, 2), 3: (3, 2)}


def blocks_of(part):
    outer = _KEEP[part] + _SEND[part]
    if part < 2:
        return [(a, b) for a in outer for b in outer]
    return [(b, a) for a in outer for b in outer]


def block_start(kx, ky):
    place = lax.axis_index("batch")
    x, y = lax.div(place, 4), lax.rem(place, 4)
    return pl.multiple_of(lax.bitwise_xor(x, kx) * 64 + lax.bitwise_xor(y, ky) * 16, 16)


def stats_kernel(
    f_hbm, c_hbm, dir_hbm, t_hbm, ub_ref, ut_ref, inv_ref, colsum_ref, stat_ref,
    f_ref, c_ref, dbuf, tbuf, sacc, macc, tacc, fsem, csem, dsem, tsem,
):
    rows = f_ref.shape[0]
    protos = dbuf.shape[1]
    tiles = protos // STAT_TILE

    def copies(n):
        cols = pl.ds(pl.multiple_of(n * STAT_TILE, STAT_TILE), STAT_TILE)
        return (
            pltpu.make_async_copy(dir_hbm.at[:, cols], dbuf.at[:, cols], dsem.at[n]),
            pltpu.make_async_copy(t_hbm.at[:, cols], tbuf.at[:, cols], tsem.at[n]),
        )

    f_copy = pltpu.make_async_copy(f_hbm, f_ref, fsem)
    c_copy = pltpu.make_async_copy(c_hbm, c_ref, csem)
    f_copy.start()
    for n in range(tiles):
        for copy in copies(n):
            copy.start()
        if n == 0:
            c_copy.start()
    f_copy.wait()
    zf = f_ref[...].astype(F32)
    inv = 1.0 / jnp.sqrt(jnp.sum(zf * zf, axis=-1, keepdims=True) + EPS)
    ub = (zf * inv).astype(BF16)
    ub_ref[...] = ub
    ut_ref[...] = ub.T
    sacc[...] = jnp.zeros_like(sacc)
    macc[...] = jnp.full_like(macc, -1e30)
    tacc[...] = jnp.zeros_like(tacc)
    colsum_ref[...] = jnp.zeros_like(colsum_ref)

    c_copy.wait()

    @pl.loop(0, tiles)
    def _(n):
        for copy in copies(n):
            copy.wait()
        cols = pl.ds(pl.multiple_of(n * STAT_TILE, STAT_TILE), STAT_TILE)
        d = dbuf[:, cols].astype(F32)
        inv_col = 1.0 / jnp.sqrt(jnp.sum(d * d, axis=0, keepdims=True) + EPS)
        inv_ref[:, cols] = inv_col
        wb = (d * inv_col).astype(BF16)
        part = None
        for k in range(STAT_TILE // STAT_SUB):
            s = jnp.dot(
                ub_ref[...], wb[:, k * STAT_SUB : (k + 1) * STAT_SUB], preferred_element_type=F32
            )
            e = jnp.exp2(s * STUDENT_C)
            for m in range(STAT_SUB // 128):
                lane = e[:, m * 128 : (m + 1) * 128]
                part = lane if part is None else part + lane
        sacc[...] += part
        t = tbuf[:, cols].astype(F32)
        ones = jnp.ones((8, tbuf.shape[0]), BF16)
        sums = jnp.dot(ones, tbuf[:, cols], preferred_element_type=F32)
        colsum_ref[pl.ds(n, 1), :] = sums[:1]
        diff = t - c_ref[:, cols]
        lanes = [diff[:, m * 128 : (m + 1) * 128] for m in range(STAT_TILE // 128)]
        old = macc[...]
        top = functools.reduce(jnp.maximum, lanes, old)
        total = tacc[...] * jnp.exp2((old - top) * TEACHER_C)
        for lane in lanes:
            total += jnp.exp2((lane - top) * TEACHER_C)
        macc[...] = top
        tacc[...] = total

    stat_ref[...] = jnp.zeros_like(stat_ref)
    for r in range(rows // 128):
        stat_ref[r : r + 1, :] = jnp.sum(sacc[r * 128 : (r + 1) * 128, :].T, axis=0, keepdims=True)
    tops = macc[...].T
    best = jnp.max(tops, axis=0, keepdims=True)
    stat_ref[5:6, :] = best
    stat_ref[6:7, :] = jnp.sum(
        tacc[...].T * jnp.exp2((tops - best) * TEACHER_C), axis=0, keepdims=True
    )


def weight_kernel(images, call, *refs):
    refs = list(refs)
    take = lambda n: [refs.pop(0) for _ in range(n)]
    first, last = call == 0, call == CALLS - 1
    ub_ref, ut_ref, dir_ref, inv_ref, t_ref, c_ref = take(6)
    stat_ref, colsum_ref = take(2) if first else (None, None)
    arow, brow, mrow, before_ref = take(4) if not first else (None,) * 4
    (f_ref,) = take(1) if last else (None,)
    keep_refs, send_refs = take(PARTS), take(PARTS)
    fouts = take(2 if last else 1)
    rows = ub_ref.shape[0]
    img = rows // 10
    if first:
        arow, brow, mrow = take(3)
        scale = 1.0 / (0.1 * 18.0 * images)
        stat = stat_ref[...]
        sums = jnp.sum(stat, axis=0)
        top = jnp.max(stat[:, 5:6, :], axis=0)
        ttot = jnp.sum(stat[:, 6:7, :] * jnp.exp2((stat[:, 5:6, :] - top) * TEACHER_C), axis=0)
        packed = jnp.concatenate([sums[0:5], top, ttot, jnp.zeros((121, 128), F32)], axis=0).T
        for r in range(5):
            arow[r * 128 : (r + 1) * 128, :] = jnp.broadcast_to(
                (scale if r == 0 else 2.0 * scale) / packed[:, r : r + 1], (128, 128)
            )
        mrow[...] = jnp.broadcast_to(packed[:, 5:6], (128, 128))
        brow[...] = jnp.broadcast_to(scale / packed[:, 6:7], (128, 128))
    ub = ub_ref[...]
    protos = dir_ref.shape[1]
    width = protos // PARTS // CALLS
    wide = lambda v: jnp.concatenate([v] * (SUB // 128), axis=1)
    total = None
    for part in range(PARTS):
        ut = jnp.concatenate(
            [ut_ref[pl.ds(block_start(kx, ky), 16), :] for kx, ky in blocks_of(part)], axis=0
        )
        base = (part * CALLS + call) * width
        for at in range(0, width, SUB):
            cols, mine = slice(at, at + SUB), slice(base + at, base + at + SUB)
            inv = inv_ref[:, mine]
            wb = (dir_ref[:, mine].astype(F32) * inv).astype(BF16)
            s = jnp.dot(ub, wb, preferred_element_type=F32)
            diff = t_ref[:, mine].astype(F32) - c_ref[:, mine]
            t = jnp.exp2((diff - wide(mrow[...])) * TEACHER_C) * wide(brow[...])
            t0, t1 = t[:img], t[img:]
            both = t0 + t1
            rounded = []
            for j in range(10):
                r = slice(j * img, (j + 1) * img)
                target = t1 if j == 0 else t0 if j == 1 else both
                rounded.append(
                    (jnp.exp2(s[r] * STUDENT_C) * wide(arow[r, :]) - target).astype(BF16)
                )
            g = jnp.concatenate(rounded, axis=0)
            gw = jnp.dot(ut, g, preferred_element_type=F32)
            term = lax.dot_general(g, wb, (((1,), (1,)), ((), ())), preferred_element_type=F32)
            total = term if total is None else total + term
            ds = []
            dots = jnp.zeros((16, SUB), F32)
            for n, (kx, ky) in enumerate(blocks_of(part)):
                d = dir_ref[pl.ds(block_start(kx, ky), 16), mine].astype(F32)
                ds.append(d)
                dots += gw[n * 16 : (n + 1) * 16] * d
            factor = jnp.sum(dots, axis=0, keepdims=True) * inv * inv * inv
            for n in range(16):
                ref, row = (keep_refs[part], n * 16) if n < 8 else (send_refs[part], (n - 8) * 16)
                ref[row : row + 16, cols] = gw[n * 16 : (n + 1) * 16] * inv - ds[n] * factor
    if first:
        send_refs[0][128:136, :] = colsum_ref[...]
    else:
        total = before_ref[...] + total
    if not last:
        fouts[0][...] = total
        return
    (acc,) = take(1)
    zf = f_ref[...].astype(F32)
    inv = 1.0 / jnp.sqrt(jnp.sum(zf * zf, axis=-1, keepdims=True) + EPS)
    unit = zf * inv
    acc[...] = (total - unit * jnp.sum(total * unit, axis=-1, keepdims=True)) * inv
    half = rows // 2
    core = lax.rem(lax.axis_index("proto"), 2)
    fouts[0][...] = acc[pl.ds(pl.multiple_of(core * half, 8), half), :]
    fouts[1][...] = acc[pl.ds(pl.multiple_of((1 - core) * half, 8), half), :]


def final_kernel(images, c_ref, cs_ref, csgot_ref, mine_ref, other_ref, *refs):
    keeps, gots = refs[: PARTS * CALLS], refs[PARTS * CALLS : PARTS * CALLS + PARTS]
    feat_ref, dir_ref, center_ref = refs[PARTS * CALLS + PARTS :]
    half = mine_ref.shape[0]
    core = lax.rem(lax.axis_index("proto"), 2)
    feat_ref[pl.ds(pl.multiple_of(core * half, 8), half), :] = mine_ref[...]
    feat_ref[pl.ds(pl.multiple_of((1 - core) * half, 8), half), :] = other_ref[...]
    width = keeps[0].shape[1]
    for part in range(PARTS):
        for call in range(CALLS):
            n = part * CALLS + call
            got = gots[part][call * 16 : (call + 1) * 16, :]
            dir_ref[:, n * width : (n + 1) * width] = keeps[n][...] + got
    cs = cs_ref[...] + csgot_ref[...]
    for n in range(8):
        cols = slice(n * STAT_TILE, (n + 1) * STAT_TILE)
        center_ref[:, cols] = 0.9 * c_ref[:, cols] + 0.1 * cs[n : n + 1, :] / (2.0 * images)


IN_VMEM = pl.BlockSpec(memory_space=pltpu.VMEM)


def params(mib):
    return pltpu.CompilerParams(vmem_limit_bytes=mib * 1024 * 1024)


def stats_call(f, dirs, teach, center):
    rows, dim = f.shape
    protos = dirs.shape[1]
    trows = teach.shape[0]
    tiles = protos // STAT_TILE
    return pl.pallas_call(
        stats_kernel,
        in_specs=[pl.BlockSpec(memory_space=pltpu.HBM)] * 4,
        out_specs=[IN_VMEM] * 5,
        scratch_shapes=[
            pltpu.VMEM((rows, dim), BF16),
            pltpu.VMEM((1, protos), F32),
            pltpu.VMEM((dim, protos), BF16),
            pltpu.VMEM((trows, protos), BF16),
            pltpu.VMEM((rows, 128), F32),
            pltpu.VMEM((trows, 128), F32),
            pltpu.VMEM((trows, 128), F32),
            pltpu.SemaphoreType.DMA,
            pltpu.SemaphoreType.DMA,
            pltpu.SemaphoreType.DMA((tiles,)),
            pltpu.SemaphoreType.DMA((tiles,)),
        ],
        out_shape=[
            jax.ShapeDtypeStruct((rows, dim), BF16),
            jax.ShapeDtypeStruct((dim, rows), BF16),
            jax.ShapeDtypeStruct((1, protos), F32),
            jax.ShapeDtypeStruct((8, STAT_TILE), F32),
            jax.ShapeDtypeStruct((8, 128), F32),
        ],
        compiler_params=params(53),
        cost_estimate=pl.CostEstimate(
            flops=2 * rows * dim * protos,
            bytes_accessed=2 * (dim + trows) * protos,
            transcendentals=(rows + trows) * protos,
        ),
        name="stats",
    )(f, center, dirs, teach)


def weight_call(images, call, ub, ut, dirs, inv, teach, center, extra):
    rows, dim = ub.shape
    protos = dirs.shape[1]
    trows = teach.shape[0]
    width = protos // PARTS // CALLS
    first, last = call == 0, call == CALLS - 1
    shape = lambda *dims: jax.ShapeDtypeStruct(dims, F32)
    outs = [shape(128, width)] * PARTS
    outs += [shape(136 if first and part == 0 else 128, width) for part in range(PARTS)]
    outs += [shape(rows // 2, dim)] * 2 if last else [shape(rows, dim)]
    outs += [shape(rows, 128), shape(trows, 128), shape(trows, 128)] if first else []
    args = [ub, ut, dirs, inv, teach, center, *extra]
    out = pl.pallas_call(
        functools.partial(weight_kernel, images, call),
        in_specs=[IN_VMEM] * len(args),
        out_specs=[IN_VMEM] * len(outs),
        scratch_shapes=[pltpu.VMEM((rows, dim), F32)] if last else [],
        out_shape=outs,
        compiler_params=params(8),
        cost_estimate=pl.CostEstimate(
            flops=6 * rows * dim * protos // CALLS,
            bytes_accessed=(2 * (dim + trows) + 4 * dim) * protos // CALLS,
            transcendentals=(rows + trows) * protos // CALLS,
        ),
        name="weights",
    )(*args)
    return out[:PARTS], out[PARTS : 2 * PARTS], out[2 * PARTS :]


def final_call(images, center, cs, csgot, mine, other, keeps, gots):
    half, dim = mine.shape
    protos = center.shape[1]
    args = [center, cs, csgot, mine, other, *keeps, *gots]
    return pl.pallas_call(
        functools.partial(final_kernel, images),
        in_specs=[IN_VMEM] * len(args),
        out_specs=[IN_VMEM] * 3,
        out_shape=[
            jax.ShapeDtypeStruct((2 * half, dim), F32),
            jax.ShapeDtypeStruct((16, protos), F32),
            jax.ShapeDtypeStruct((1, protos), F32),
        ],
        compiler_params=params(8),
        name="final",
    )(*args)


def pairs_x(k):
    return [(x * 4 + y, (x ^ k) * 4 + y) for x in range(4) for y in range(4)]


def pairs_y(k):
    return [(x * 4 + y, x * 4 + (y ^ k)) for x in range(4) for y in range(4)]


X1, X3, Y1, Y3 = pairs_x(1), pairs_x(3), pairs_y(1), pairs_y(3)
ORDER = [(X1, X3, Y1, Y3), (X3, X1, Y3, Y1), (Y1, Y3, X1, X3), (Y3, Y1, X3, X1)]


def on_device(features, teacher_logits, directions, center):
    crops, img, dim = features.shape
    images = img * lax.axis_size("batch")
    protos = directions.shape[1]
    rows = crops * img
    f = features.reshape(rows, dim)
    teach = teacher_logits.reshape(-1, protos)
    cent = center.reshape(1, protos)
    ub, ut, inv, colsum, stat = stats_call(f, directions, teach, cent)
    stats = lax.all_to_all(jnp.broadcast_to(stat, (8, 8, 128)), "proto", 0, 0)
    keeps, sends, extra = [], [], [stats, colsum]
    for call in range(CALLS):
        if call == CALLS - 1:
            extra = extra + [f]
        keep, send, rest = weight_call(images, call, ub, ut, directions, inv, teach, cent, extra)
        factors = rest[1:] if call == 0 else factors
        extra = [*factors, rest[0]]
        keeps.append(keep)
        sends.append([lax.ppermute(send[p], "batch", ORDER[p][0]) for p in range(PARTS)])
    fkeep, fsend = rest
    cs, before = colsum, None
    got = [[None] * CALLS for _ in range(PARTS)]
    for call in range(CALLS):
        for part in range(PARTS):
            block = sends[call][part]
            if before is not None:
                block, _ = lax.optimization_barrier((block, before))
            before = block
            got[part][call] = block[:128]
            if call == 0 and part == 0:
                fsend, _ = lax.optimization_barrier((fsend, block))
            if call == 0 and part == 0:
                cs = cs + block[128:]
    keeps = [[keeps[call][part] for call in range(CALLS)] for part in range(PARTS)]
    for n in (1, 2, 3):
        size = 128 >> n
        arrived, before = [], None
        for part in range(PARTS):
            out = [keeps[part][c][size:] + got[part][c][size:] for c in range(CALLS)]
            out += [cs] if part == 0 else []
            keeps[part] = [keeps[part][c][:size] + got[part][c][:size] for c in range(CALLS)]
            block = lax.ppermute(jnp.concatenate(out, axis=0), "batch", ORDER[part][n])
            if before is not None:
                block, _ = lax.optimization_barrier((block, before))
            before = block
            arrived.append(block)
            got[part] = [block[c * size : (c + 1) * size] for c in range(CALLS)]
        if n < 3:
            cs = cs + arrived[0][CALLS * size :]
    total = fkeep + lax.ppermute(fsend, "proto", [(i, i ^ 1) for i in range(8)])
    total = total + lax.ppermute(total, "proto", [(i, i ^ 2) for i in range(8)])
    total = total + lax.ppermute(total, "proto", [(i, i ^ 6) for i in range(8)])
    other = lax.ppermute(total, "proto", [(i, i ^ 1) for i in range(8)])
    keeps = [keeps[part][call] for part in range(PARTS) for call in range(CALLS)]
    csgot = arrived[0][CALLS * 16 :]
    grad_features, grad_directions, new_center = final_call(
        images, cent, cs, csgot, total, other, keeps, arrived
    )
    return (
        grad_features.reshape(crops, img, dim),
        grad_directions,
        new_center.reshape(protos),
    )


def solution(mesh):
    in_specs = (P(None, "batch", None), P(None, "batch", "proto"), P(None, "proto"), P("proto"))
    out_specs = (P(None, "batch", None), P("batch", "proto"), P("proto"))
    return jax.shard_map(
        on_device, mesh=mesh, in_specs=in_specs, out_specs=out_specs, check_vma=False
    )
```
